32 devices in a mesh: section: 4 (over x, core), expert: 8 (over z, y).
Axes of the slice: x: 2, y: 2, z: 4, core: 2. Of those that a mesh axis runs over, the one named last changes fastest.
Arguments:
- inputs: bfloat16 [4, 256, 4096], P(None, 'expert'), may hold values from -6 to 6
- cotangent: bfloat16 [4, 256, 4096], P(None, 'expert'), may hold values from -6 to 6
- gain: float32 [4, 4096], P('section'), may hold values from 0.25 to 1.75
- route: int32 [4, 4, 256, 2], P('section', None, 'expert'), may hold values from 0 to 7, all different within a row; in each aligned block of 32 rows (0 to 31, 32 to 63, ..., all dimensions but the last counted through in order) at most 9 rows name the same one
- gate: float32 [4, 4, 256, 2], P('section', None, 'expert'), may hold values from 0.3 to 1
- w_gate: bfloat16 [4, 8, 4096, 768], P('section', 'expert'), may hold values from -0.09375 to 0.09375
- w_up: bfloat16 [4, 8, 4096, 768], P('section', 'expert'), may hold values from -0.09375 to 0.09375
- w_down: bfloat16 [4, 8, 768, 4096], P('section', 'expert'), may hold values from -0.21875 to 0.21875
Outputs:
- hidden: bfloat16 [4, 4, 256, 4096], P('section', None, 'expert')
- grads: bfloat16 [4, 4, 256, 4096], P('section', None, 'expert')
The draws below stay inside these ranges and needn't reach their ends.
Inputs may be any that keep to these rules, and one draw needn't show every extreme that they name: `route`: each token names 2 different experts. Among the 32 tokens that one device holds of one micro-batch in one section, no expert is named by more than 9 tokens, a bound that some block reaches.
All inputs are finite; a program needn't handle non-finite values.
Results may differ from the reference program's by a relative error of at most 0.03.
Values may be sent and summed in bfloat16 or wider, within the bound.
A program may use at most 64 MiB of HBM per device.

```python
import math
import jax
import jax.numpy as jnp
import numpy as np
from jax import lax

D = 4096
HID = 768
TOP = 2
MICRO = 4
TOK_MB = 32
EXPERTS = 8
SECTIONS = 4
TOKENS = 256
CAP = 9
N_EXPERT = 8


def level_of(stream_key, extent, split, least, high):
    level = 1.0
    for axis_at, blocks in split:
        heights = jax.random.uniform(jax.random.fold_in(jax.random.fold_in(stream_key, 6), axis_at), (blocks,), jnp.float32, least / len(split), high / len(split))
        level = level * jnp.repeat(jnp.exp(heights), extent[axis_at] // blocks).reshape((-1,) + (1,) * (len(extent) - 1 - axis_at))
    return level


def routed_block(own_key, own, number, rows, amount, top, bound, skew):
    sequence = jax.random.permutation(own_key, amount)
    packed, common = portions_of(amount, rows * top, bound, skew, True), portions_of(amount, rows * top, bound, skew, False)
    places = jnp.arange(amount)

    def named(lengths, rotation):
        used = int((lengths > 0).sum())
        fixed = max(1, used // 4)
        shifted = fixed + (places - fixed + rotation * (used - fixed)) % max(1, amount - fixed)
        return jnp.zeros((amount,), jnp.int32).at[sequence[jnp.where(places < fixed, places, shifted)]].set(jnp.asarray(lengths, jnp.int32))

    lengths = jnp.where(number % 4 == 0, named(packed, number // 4), named(common, number - number // 4 - 1))
    mixed = jax.random.permutation(jax.random.fold_in(own, 3), amount)
    giver, sink = mixed[0:amount // 2 * 2:2], mixed[1:amount // 2 * 2:2]
    slack = jnp.minimum(lengths[giver] - 1, bound - lengths[sink]) // 2
    slack = jnp.where((giver == sequence[0]) | (sink == sequence[0]) | (lengths[sink] == 0), 0, jnp.maximum(slack, 0))
    shifted = jax.random.randint(jax.random.fold_in(own, 4), (amount // 2,), 0, 1 << 20) % (slack + 1)
    lengths = lengths.at[giver].add(-shifted).at[sink].add(shifted)
    members = jnp.searchsorted(jnp.cumsum(lengths), jnp.arange(rows * top), side="right").astype(jnp.int32)
    grid = members.reshape(top, rows).T
    grid = grid[jax.random.permutation(jax.random.fold_in(own, 1), rows)]
    rotation = jax.random.randint(jax.random.fold_in(own, 2), (rows, 1), 0, top)
    return jnp.take_along_axis(grid, (jnp.arange(top)[None, :] + rotation) % top, axis=1)


def portions_of(amount, total, bound, lean, full):
    weights = [(1 << 20) // math.isqrt(standing ** lean) + 1 for standing in range(1, amount + 1)]
    largest = bound if full else min(bound, max(-(-total // amount), total * weights[0] // sum(weights)))
    least = 1 if total - largest >= amount - 1 else 0
    holding, spare = [largest] + [least] * (amount - 1), total - largest - least * (amount - 1)
    while spare > 0:
        movable = [i for i in range(1, amount) if holding[i] < largest] or [i for i in range(1, amount) if holding[i] < bound]
        whole, remaining = sum([weights[i] for i in movable]), spare
        for i in movable:
            extra = min(bound - holding[i], max(1, remaining * weights[i] // whole), spare)
            holding[i] = holding[i] + extra
            spare = spare - extra
    return np.array(holding)


def centred(key, shape, spread, bound, split=(), kind=jnp.bfloat16):
    values = jax.random.normal(key, shape, jnp.float32) * spread
    if len(split) > 0:
        values = level_of(key, shape, split, -0.22, 0.18) * values
    return jnp.clip(values, min=-bound, max=bound).astype(kind)


def setup_inputs(seed: int = 0) -> dict:
    arg_keys = jax.random.split(jax.random.key(seed), 9)
    inputs = centred(arg_keys[0], (MICRO, TOKENS, D), 1.0, 6.0, ((1, 8),))
    cotangent = centred(arg_keys[1], (MICRO, TOKENS, D), 1.0, 6.0, ((1, 8),))
    gain = jnp.clip(1.0 + 0.15 * jax.random.normal(arg_keys[2], (SECTIONS, D), jnp.float32), 0.25, 1.75)
    route_keys = jax.random.split(jax.random.fold_in(arg_keys[3], 1), SECTIONS * MICRO * TOKENS // TOK_MB)
    route_turns = jax.random.permutation(jax.random.fold_in(arg_keys[3], 3), SECTIONS * MICRO * TOKENS // TOK_MB)
    route = jax.vmap(lambda own, number: routed_block(jax.random.fold_in(arg_keys[3], 2), own, number, TOK_MB, EXPERTS, TOP, CAP, 2))(route_keys, route_turns).reshape((SECTIONS, MICRO, TOKENS, TOP))
    gate = jnp.clip(0.3 + 0.7 * jax.random.uniform(arg_keys[4], (SECTIONS, MICRO, TOKENS, TOP), jnp.float32) ** level_of(arg_keys[4], (SECTIONS, MICRO, TOKENS, TOP), ((0, 4), (2, 8)), -0.2, 0.2), 0.3, 1.0)
    w_gate = centred(arg_keys[5], (SECTIONS, EXPERTS, D, HID), D ** -0.5, 0.09375, ((0, 4), (1, 8)))
    w_up = centred(arg_keys[6], (SECTIONS, EXPERTS, D, HID), D ** -0.5, 0.09375, ((0, 4), (1, 8)))
    w_down = centred(arg_keys[7], (SECTIONS, EXPERTS, HID, D), HID ** -0.5, 0.21875, ((0, 4), (1, 8)))
    return {"inputs": inputs, "cotangent": cotangent, "gain": gain, "route": route, "gate": gate, "w_gate": w_gate, "w_up": w_up, "w_down": w_down}


EPS = 1e-06

def block_positions(route):
    blocks = route.reshape(N_EXPERT, TOK_MB * TOP)
    onehot = (blocks[:, :, None] == jnp.arange(EXPERTS, dtype=jnp.int32)[None, None, :]).astype(jnp.int32)
    before = jnp.cumsum(onehot, axis=1) - onehot
    slot = lax.optimization_barrier(jnp.sum(before * onehot, axis=2)).astype(jnp.int32)
    source = jnp.arange(N_EXPERT, dtype=jnp.int32)[:, None]
    return (source * CAP + slot).reshape(route.shape).astype(jnp.int32)

def normalize(tokens, gain):
    values = tokens.astype(jnp.float32)
    scale = lax.rsqrt(lax.optimization_barrier(jnp.mean(values * values, axis=-1, keepdims=True)) + EPS)
    return (values, scale, (values * scale * gain).astype(jnp.bfloat16))

def expert_rows(rows, route, place):
    empty = jnp.zeros((EXPERTS, N_EXPERT * CAP, D), jnp.bfloat16)
    return empty.at[route.reshape(-1), place.reshape(-1)].set(rows.reshape(-1, D))

def forward_experts(buffers, w_gate, w_up, w_down):

    def single(operands):
        rows, weight_gate, weight_up, weight_down = operands
        pre_gate = jnp.dot(rows, weight_gate, preferred_element_type=jnp.float32)
        pre_up = jnp.dot(rows, weight_up, preferred_element_type=jnp.float32)
        product = (pre_gate * jax.nn.sigmoid(pre_gate) * pre_up).astype(jnp.bfloat16)
        output = jnp.dot(product, weight_down, preferred_element_type=jnp.float32).astype(jnp.bfloat16)
        return (output, pre_gate, pre_up)
    return lax.map(single, (buffers, w_gate, w_up, w_down))

def section_forward(tokens, gain, route, gate, w_gate, w_up, w_down):
    values, scale, normed = normalize(tokens, gain)
    place = block_positions(route)
    rows = jnp.broadcast_to(normed[:, None, :], (TOKENS, TOP, D))
    output, pre_gate, pre_up = forward_experts(expert_rows(rows, route, place), w_gate, w_up, w_down)
    picked = output[route, place]
    mixed = values + lax.optimization_barrier(jnp.sum(gate[..., None] * picked.astype(jnp.float32), axis=1))
    return mixed.astype(jnp.bfloat16)

def section_backward(tokens, grad_out, gain, route, gate, w_gate, w_up, w_down):
    values, scale, normed = normalize(tokens, gain)
    place = block_positions(route)
    rows = jnp.broadcast_to(normed[:, None, :], (TOKENS, TOP, D))
    output, pre_gate, pre_up = forward_experts(expert_rows(rows, route, place), w_gate, w_up, w_down)
    scaled = (gate[..., None] * grad_out.astype(jnp.float32)[:, None, :]).astype(jnp.bfloat16)
    grad_rows = expert_rows(scaled, route, place)

    def single(operands):
        grad_block, gate_pre, up_pre, weight_gate, weight_up, weight_down = operands
        d_hidden = jnp.dot(grad_block, weight_down.T, preferred_element_type=jnp.float32)
        sigma = jax.nn.sigmoid(gate_pre)
        d_gate = (d_hidden * up_pre * sigma * (1.0 + gate_pre * (1.0 - sigma))).astype(jnp.bfloat16)
        d_up = (d_hidden * gate_pre * sigma).astype(jnp.bfloat16)
        back = jnp.dot(d_gate, weight_gate.T, preferred_element_type=jnp.float32) + jnp.dot(d_up, weight_up.T, preferred_element_type=jnp.float32)
        return back.astype(jnp.bfloat16)
    back = lax.map(single, (grad_rows, pre_gate, pre_up, w_gate, w_up, w_down))
    d_norm = lax.optimization_barrier(jnp.sum(back[route, place].astype(jnp.float32), axis=1))
    weighted = d_norm * gain
    result = grad_out.astype(jnp.float32) + scale * weighted - values * (scale * scale * scale) * lax.optimization_barrier(jnp.mean(values * weighted, axis=-1, keepdims=True))
    return result.astype(jnp.bfloat16)

def reference(inputs, cotangent, gain, route, gate, w_gate, w_up, w_down):

    def forward(current, per_section):
        gain_s, route_s, gate_s, wg, wu, wd = per_section
        produced = lax.map(lambda item: section_forward(item[0], gain_s, item[1], item[2], wg, wu, wd), (current, route_s, gate_s))
        return (produced, produced)
    _, hidden = lax.scan(forward, inputs, (gain, route, gate, w_gate, w_up, w_down))
    section_inputs = jnp.concatenate([inputs[None], hidden[:-1]], axis=0)

    def backward(grad_now, per_section):
        inputs_s, gain_s, route_s, gate_s, wg, wu, wd = per_section
        produced = lax.map(lambda item: section_backward(item[0], item[1], gain_s, item[2], item[3], wg, wu, wd), (inputs_s, grad_now, route_s, gate_s))
        return (produced, produced)
    _, grads = lax.scan(backward, cotangent, (section_inputs, gain, route, gate, w_gate, w_up, w_down), reverse=True)
    return (hidden, grads)
```

```python
import functools

import jax
import jax.numpy as jnp
from jax import lax
from jax.experimental import pallas as pl
from jax.experimental.pallas import tpu as pltpu
from jax.sharding import PartitionSpec as P

EPS = 1e-06
MESH = pl.DeviceIdType.MESH
PIECE = 256
FOLD = 16
F32 = jnp.float32
BF16 = jnp.bfloat16


def mm(left, right):
    return jnp.dot(left, right, preferred_element_type=F32)


def mm_last(left, right):
    return lax.dot_general(left, right, (((1,), (1,)), ((), ())), preferred_element_type=F32)


def onehot(condition):
    return jnp.where(condition, 1.0, 0.0).astype(F32)


def kernel(
    experts, sections, capacity,
    inputs, cotangent, gain, route, route_t, gate, w_gate, w_up, w_down,
    hidden, grads,
    wg, wu, wd, xin, dyin, sent, got, kept_gate, kept_up, wide, narrow, inner_a, inner_b,
    weight_sem, send_sem, recv_sem, pass_send, pass_recv,
):
    micro, tok, width = inputs.shape
    inner = wg.shape[1]
    rows = experts * capacity
    block = capacity * FOLD
    pieces = width // PIECE
    section = lax.axis_index("section")
    me = lax.axis_index("expert")

    weight_copies = [
        pltpu.make_async_copy(source, target, weight_sem.at[i])
        for i, (source, target) in enumerate(((w_gate, wg), (w_up, wu), (w_down, wd)))
    ]
    for copy in weight_copies:
        copy.start()

    barrier = pltpu.get_barrier_semaphore()
    for d in range(1, experts):
        pl.semaphore_signal(
            barrier, inc=1, device_id={"expert": lax.rem(me + d, experts)}, device_id_type=MESH
        )
    for d in (1, sections - 1):
        pl.semaphore_signal(
            barrier, inc=1, device_id={"section": lax.rem(section + d, sections)},
            device_id_type=MESH,
        )

    @pl.when(section == 0)
    def _():
        xin[...] = inputs[...]

    @pl.when(section == sections - 1)
    def _():
        dyin[...] = cotangent[...]

    pl.semaphore_wait(barrier, experts + 1)

    def part(e):
        return pl.ds(pl.multiple_of(e * block, 16), block)

    def exchange(kind, m, peer):
        return pltpu.make_async_remote_copy(
            src_ref=sent.at[kind, m, part(peer)],
            dst_ref=got.at[kind, m, part(me)],
            send_sem=send_sem.at[kind, m, peer],
            recv_sem=recv_sem.at[kind, m, me],
            device_id={"expert": peer},
            device_id_type=MESH,
        )

    def arrival(kind, m, peer):
        return pltpu.make_async_remote_copy(
            src_ref=sent.at[kind, m, part(me)],
            dst_ref=got.at[kind, m, part(peer)],
            send_sem=send_sem.at[kind, m, me],
            recv_sem=recv_sem.at[kind, m, peer],
            device_id={"expert": peer},
            device_id_type=MESH,
        )

    def ship(kind, m):
        for d in range(1, experts):
            exchange(kind, m, lax.rem(me + d, experts)).start()
        got[kind, m, part(me), :] = sent[kind, m, part(me), :]

    def collect(kind, m):
        for d in range(1, experts):
            arrival(kind, m, lax.rem(me + d, experts)).wait_recv()

    def hidden_pass(m):
        return pltpu.make_async_remote_copy(
            src_ref=hidden.at[m], dst_ref=xin.at[m],
            send_sem=pass_send.at[0, m], recv_sem=pass_recv.at[0, m],
            device_id={"section": lax.rem(section + 1, sections)}, device_id_type=MESH,
        )

    def grads_pass(m):
        return pltpu.make_async_remote_copy(
            src_ref=grads.at[m], dst_ref=dyin.at[m],
            send_sem=pass_send.at[1, m], recv_sem=pass_recv.at[1, m],
            device_id={"section": lax.rem(section + sections - 1, sections)},
            device_id_type=MESH,
        )

    span = 8 * FOLD
    row_i = lax.broadcasted_iota(jnp.int32, (span, span), 0)
    col_i = lax.broadcasted_iota(jnp.int32, (span, span), 1)

    def fold(kind, m):
        order = onehot(col_i == (row_i % FOLD) * 8 + row_i // FOLD).astype(BF16)

        def step(g, _):
            at = pl.ds(pl.multiple_of(g * 8, 8), 8)
            stack = jnp.concatenate(
                [wide[at, p * PIECE:(p + 1) * PIECE] for p in range(pieces)], axis=0
            ).astype(BF16)
            sent[kind, m, pl.ds(pl.multiple_of(g * span, span), span), :] = mm(
                order, stack
            ).astype(BF16)
            return 0

        lax.fori_loop(0, rows // 8, step, 0, unroll=True)

    def unfold(kind, m):
        order = onehot(col_i == (row_i % 8) * FOLD + row_i // 8).astype(BF16)

        def step(g, _):
            at = pl.ds(pl.multiple_of(g * 8, 8), 8)
            flat = mm(order, got[kind, m, pl.ds(pl.multiple_of(g * span, span), span), :])
            for p in range(pieces):
                wide[at, p * PIECE:(p + 1) * PIECE] = flat[p * 8:(p + 1) * 8]
            return 0

        lax.fori_loop(0, rows // 8, step, 0, unroll=True)
        narrow[...] = wide[...].astype(BF16)

    def tables_t(m):
        expert = lax.broadcasted_iota(jnp.int32, (experts, tok), 0)
        names = route_t[m]
        ohs = [onehot(names[k:k + 1] == expert) for k in range(2)]
        earlier = onehot(
            lax.broadcasted_iota(jnp.int32, (tok, tok), 0)
            < lax.broadcasted_iota(jnp.int32, (tok, tok), 1)
        )
        before = mm((ohs[0] + ohs[1]).astype(BF16), earlier.astype(BF16))
        slot = lax.broadcasted_iota(jnp.int32, (rows, tok), 0).astype(F32)
        out = []
        for k in range(2):
            place = names[k:k + 1].astype(F32) * capacity + jnp.sum(
                ohs[k] * before, axis=0, keepdims=True
            )
            out.append(onehot(slot == place))
        return out

    def tables(m):
        expert = lax.broadcasted_iota(jnp.int32, (tok, experts), 1)
        names = route[m]
        ohs = [onehot(names[:, k:k + 1] == expert) for k in range(2)]
        earlier = onehot(
            lax.broadcasted_iota(jnp.int32, (tok, tok), 1)
            < lax.broadcasted_iota(jnp.int32, (tok, tok), 0)
        )
        before = mm(earlier.astype(BF16), (ohs[0] + ohs[1]).astype(BF16))
        slot = lax.broadcasted_iota(jnp.int32, (tok, rows), 1).astype(F32)
        out = []
        for k in range(2):
            place = names[:, k:k + 1].astype(F32) * capacity + jnp.sum(
                ohs[k] * before, axis=1, keepdims=True
            )
            out.append(onehot(slot == place))
        return out

    def rms_of(values):
        return lax.rsqrt(jnp.mean(values * values, axis=-1, keepdims=True) + EPS)

    def forward_send(m):
        @pl.when(section > 0)
        def _():
            hidden_pass(m).wait_recv()

        values = xin[m].astype(F32)
        normed = (values * rms_of(values) * gain[...]).astype(BF16)
        first, second = tables_t(m)
        wide[...] = mm((first + second).astype(BF16), normed)
        fold(0, m)
        ship(0, m)

    def forward_expert(m):
        @pl.when(m == 0)
        def _():
            for copy in weight_copies:
                copy.wait()

        collect(0, m)
        unfold(0, m)

        def up(n, _):
            at = pl.ds(pl.multiple_of(n * 256, 256), 256)
            pre_gate = mm(narrow[...], wg[:, at])
            pre_up = mm(narrow[...], wu[:, at])
            kept_gate[m, :, at] = pre_gate
            kept_up[m, :, at] = pre_up
            inner_a[:, at] = (pre_gate * jax.nn.sigmoid(pre_gate) * pre_up).astype(BF16)
            return 0

        lax.fori_loop(0, inner // 256, up, 0)

        def down(n, _):
            at = pl.ds(pl.multiple_of(n * 512, 512), 512)
            wide[:, at] = mm(inner_a[...], wd[:, at])
            return 0

        lax.fori_loop(0, width // 512, down, 0)
        fold(1, m)
        ship(1, m)

    def forward_merge(m):
        collect(1, m)
        unfold(1, m)
        first, second = tables(m)
        weights = gate[m]
        mixed = (
            xin[m].astype(F32)
            + weights[:, 0:1] * mm(first.astype(BF16), narrow[...])
            + weights[:, 1:2] * mm(second.astype(BF16), narrow[...])
        )
        hidden[m] = mixed.astype(BF16)

        @pl.when(section < sections - 1)
        def _():
            hidden_pass(m).start()

    def backward_send(m):
        @pl.when(section < sections - 1)
        def _():
            grads_pass(m).wait_recv()

        grad_out = dyin[m].astype(F32)
        weights = gate[m]
        scaled = jnp.concatenate(
            [(weights[:, k:k + 1] * grad_out).astype(BF16) for k in range(2)], axis=0
        )
        table = jnp.concatenate(tables_t(m), axis=1).astype(BF16)
        wide[...] = mm(table, scaled)
        fold(2, m)
        ship(2, m)

    def backward_expert(m):
        collect(2, m)
        unfold(2, m)

        def down(n, _):
            at = pl.ds(pl.multiple_of(n * 256, 256), 256)
            d_hidden = mm_last(narrow[...], wd[at, :])
            pre_gate = kept_gate[m, :, at]
            pre_up = kept_up[m, :, at]
            sigma = jax.nn.sigmoid(pre_gate)
            inner_a[:, at] = (
                d_hidden * pre_up * sigma * (1.0 + pre_gate * (1.0 - sigma))
            ).astype(BF16)
            inner_b[:, at] = (d_hidden * pre_gate * sigma).astype(BF16)
            return 0

        lax.fori_loop(0, inner // 256, down, 0)

        def up(n, _):
            at = pl.ds(pl.multiple_of(n * 512, 512), 512)
            wide[:, at] = mm_last(inner_a[...], wg[at, :]) + mm_last(inner_b[...], wu[at, :])
            return 0

        lax.fori_loop(0, width // 512, up, 0)
        fold(3, m)
        ship(3, m)

    def backward_merge(m):
        collect(3, m)
        unfold(3, m)
        first, second = tables(m)
        values = xin[m].astype(F32)
        scale = rms_of(values)
        weighted = mm((first + second).astype(BF16), narrow[...]) * gain[...]
        result = (
            dyin[m].astype(F32)
            + scale * weighted
            - values
            * (scale * scale * scale)
            * jnp.mean(values * weighted, axis=-1, keepdims=True)
        )
        grads[m] = result.astype(BF16)

        @pl.when(section > 0)
        def _():
            grads_pass(m).start()

    def tick(t, _):
        ahead = t - section
        back = t - (2 * sections - 2 - section)

        def guarded(stage, m):
            @pl.when((m >= 0) & (m < micro))
            def _():
                stage(m)

        guarded(forward_send, ahead)
        guarded(backward_send, back)
        guarded(forward_expert, ahead)
        guarded(backward_expert, back)
        guarded(forward_merge, ahead)
        guarded(backward_merge, back)
        return 0

    lax.fori_loop(0, 2 * sections + micro - 2, tick, 0)

    def drain(m, _):
        for kind in range(4):
            for d in range(1, experts):
                exchange(kind, m, lax.rem(me + d, experts)).wait_send()

        @pl.when(section < sections - 1)
        def _():
            hidden_pass(m).wait_send()

        @pl.when(section > 0)
        def _():
            grads_pass(m).wait_send()

        return 0

    lax.fori_loop(0, micro, drain, 0)


def local(inputs, cotangent, gain, route, gate, w_gate, w_up, w_down):
    micro, tok, width = inputs.shape
    top = route.shape[-1]
    experts = lax.axis_size("expert")
    sections = lax.axis_size("section")
    capacity = tok * top * 7 // (6 * experts)
    rows = experts * capacity
    inner = w_gate.shape[-1]
    vmem = pl.BlockSpec(memory_space=pltpu.VMEM)
    hbm = pl.BlockSpec(memory_space=pl.ANY)
    shape = jax.ShapeDtypeStruct((micro, tok, width), BF16)
    hidden, grads = pl.pallas_call(
        functools.partial(kernel, experts, sections, capacity),
        out_shape=(shape, shape),
        in_specs=[vmem] * 6 + [hbm] * 3,
        out_specs=(vmem, vmem),
        scratch_shapes=[
            pltpu.VMEM((width, inner), BF16),
            pltpu.VMEM((width, inner), BF16),
            pltpu.VMEM((inner, width), BF16),
            pltpu.VMEM((micro, tok, width), BF16),
            pltpu.VMEM((micro, tok, width), BF16),
            pltpu.VMEM((4, micro, rows * FOLD, PIECE), BF16),
            pltpu.VMEM((4, micro, rows * FOLD, PIECE), BF16),
            pltpu.VMEM((micro, rows, inner), F32),
            pltpu.VMEM((micro, rows, inner), F32),
            pltpu.VMEM((rows, width), F32),
            pltpu.VMEM((rows, width), BF16),
            pltpu.VMEM((rows, inner), BF16),
            pltpu.VMEM((rows, inner), BF16),
            pltpu.SemaphoreType.DMA((3,)),
            pltpu.SemaphoreType.DMA((4, micro, experts)),
            pltpu.SemaphoreType.DMA((4, micro, experts)),
            pltpu.SemaphoreType.DMA((2, micro)),
            pltpu.SemaphoreType.DMA((2, micro)),
        ],
        compiler_params=pltpu.CompilerParams(
            collective_id=0, has_side_effects=True, vmem_limit_bytes=60 * 2**20
        ),
    )(
        inputs, cotangent, gain, route[0], jnp.swapaxes(route[0], 1, 2), gate[0],
        w_gate[0, 0], w_up[0, 0], w_down[0, 0],
    )
    return (hidden[None], grads[None])


def solution(mesh):
    placed = (
        P(None, "expert", None),
        P(None, "expert", None),
        P("section", None),
        P("section", None, "expert", None),
        P("section", None, "expert", None),
        P("section", "expert", None, None),
        P("section", "expert", None, None),
        P("section", "expert", None, None),
    )
    return jax.shard_map(
        local,
        mesh=mesh,
        in_specs=placed,
        out_specs=(P("section", None, "expert", None), P("section", None, "expert", None)),
        check_vma=False,
    )
```

```python
import functools

import jax
import jax.numpy as jnp
from jax import lax
from jax.experimental import pallas as pl
from jax.experimental.pallas import tpu as pltpu
from jax.sharding import PartitionSpec as P

EPS = 1e-06
MESH = pl.DeviceIdType.MESH
FOLD = 16
PARTS = 2
F32 = jnp.float32
BF16 = jnp.bfloat16


def mm(left, right):
    return jnp.dot(left, right, preferred_element_type=F32)


def mm_last(left, right):
    return lax.dot_general(left, right, (((1,), (1,)), ((), ())), preferred_element_type=F32)


def onehot(condition):
    return jnp.where(condition, 1.0, 0.0).astype(F32)


def kernel(
    experts, sections, capacity,
    inputs, cotangent, gain, routing, w_gate, w_up, w_down,
    hidden, grads,
    wg, wu, wd, xin, dyin, sent, got, kept_gate, kept_up, d_inner, wide, narrow,
    inner_p, inner_a, inner_b, pick, place,
    weight_sem, send_sem, recv_sem, pass_send, pass_recv,
):
    micro, tok, width = inputs.shape
    inner = wg.shape[1]
    rows = experts * capacity
    block = capacity * FOLD
    part_width = width // PARTS
    piece = part_width // FOLD
    section = lax.axis_index("section")
    me = lax.axis_index("expert")
    last = section == sections - 1
    parts = [slice(h * part_width, (h + 1) * part_width) for h in range(PARTS)]

    weight_copies = [
        pltpu.make_async_copy(source, target, weight_sem.at[i])
        for i, (source, target) in enumerate(((w_gate, wg), (w_up, wu), (w_down, wd)))
    ]
    for copy in weight_copies:
        copy.start()

    barrier = pltpu.get_barrier_semaphore()
    for d in range(1, experts):
        pl.semaphore_signal(
            barrier, inc=1, device_id={"expert": lax.rem(me + d, experts)}, device_id_type=MESH
        )
    for d in (1, sections - 1):
        pl.semaphore_signal(
            barrier, inc=1, device_id={"section": lax.rem(section + d, sections)},
            device_id_type=MESH,
        )

    @pl.when(section == 0)
    def _():
        xin[...] = inputs[...]

    @pl.when(last)
    def _():
        dyin[...] = cotangent[...]

    every = micro * tok
    expert_i = lax.broadcasted_iota(jnp.int32, (every, experts), 1).astype(F32)
    ohs = [onehot(routing[:, k:k + 1] == expert_i) for k in range(2)]
    row_t = lax.broadcasted_iota(jnp.int32, (every, every), 0)
    col_t = lax.broadcasted_iota(jnp.int32, (every, every), 1)
    earlier = onehot((col_t < row_t) & (col_t // tok == row_t // tok))
    before = mm(earlier.astype(BF16), (ohs[0] + ohs[1]).astype(BF16))
    slot = lax.broadcasted_iota(jnp.int32, (every, 128), 1).astype(F32)
    for k in range(2):
        at_row = routing[:, k:k + 1] * capacity + jnp.sum(
            ohs[k] * before, axis=1, keepdims=True
        )
        table = onehot(slot == at_row)
        table_t = table.T
        for m in range(micro):
            pick[k, m] = table[m * tok:(m + 1) * tok, :rows].astype(BF16)
            place[k, m] = table_t[:rows, m * tok:(m + 1) * tok].astype(BF16)

    pl.semaphore_wait(barrier, experts + 1)

    def rows_of(e):
        return pl.ds(pl.multiple_of(e * block, 16), block)

    def exchange(kind, m, h, peer):
        return pltpu.make_async_remote_copy(
            src_ref=sent.at[kind, m, h, rows_of(peer)],
            dst_ref=got.at[kind, m, h, rows_of(me)],
            send_sem=send_sem.at[kind, m, h, peer],
            recv_sem=recv_sem.at[kind, m, h, me],
            device_id={"expert": peer},
            device_id_type=MESH,
        )

    def arrival(kind, m, h, peer):
        return pltpu.make_async_remote_copy(
            src_ref=sent.at[kind, m, h, rows_of(me)],
            dst_ref=got.at[kind, m, h, rows_of(peer)],
            send_sem=send_sem.at[kind, m, h, me],
            recv_sem=recv_sem.at[kind, m, h, peer],
            device_id={"expert": peer},
            device_id_type=MESH,
        )

    def hidden_pass(m, h):
        return pltpu.make_async_remote_copy(
            src_ref=hidden.at[m, :, parts[h]], dst_ref=xin.at[m, :, parts[h]],
            send_sem=pass_send.at[0, m, h], recv_sem=pass_recv.at[0, m, h],
            device_id={"section": lax.rem(section + 1, sections)}, device_id_type=MESH,
        )

    def grads_pass(m, h):
        return pltpu.make_async_remote_copy(
            src_ref=grads.at[m, :, parts[h]], dst_ref=dyin.at[m, :, parts[h]],
            send_sem=pass_send.at[1, m, h], recv_sem=pass_recv.at[1, m, h],
            device_id={"section": lax.rem(section + sections - 1, sections)},
            device_id_type=MESH,
        )

    span = 8 * FOLD
    row_i = lax.broadcasted_iota(jnp.int32, (span, span), 0)
    col_i = lax.broadcasted_iota(jnp.int32, (span, span), 1)

    def ship(kind, m, h):
        order = onehot(col_i == (row_i % FOLD) * 8 + row_i // FOLD).astype(BF16)

        def step(g, _):
            at = pl.ds(pl.multiple_of(g * 8, 8), 8)
            base = h * part_width
            stack = jnp.concatenate(
                [wide[at, base + p * piece:base + (p + 1) * piece] for p in range(FOLD)], axis=0
            ).astype(BF16)
            sent[kind, m, h, pl.ds(pl.multiple_of(g * span, span), span), :] = mm(
                order, stack
            ).astype(BF16)
            return 0

        lax.fori_loop(0, rows // 8, step, 0, unroll=True)
        for d in range(1, experts):
            exchange(kind, m, h, lax.rem(me + d, experts)).start()
        got[kind, m, h, rows_of(me), :] = sent[kind, m, h, rows_of(me), :]

    def collect(kind, m, h):
        for d in range(1, experts):
            arrival(kind, m, h, lax.rem(me + d, experts)).wait_recv()
        order = onehot(col_i == (row_i % 8) * FOLD + row_i // 8).astype(BF16)

        def step(g, _):
            at = pl.ds(pl.multiple_of(g * 8, 8), 8)
            base = h * part_width
            flat = mm(order, got[kind, m, h, pl.ds(pl.multiple_of(g * span, span), span), :])
            for p in range(FOLD):
                wide[at, base + p * piece:base + (p + 1) * piece] = flat[p * 8:(p + 1) * 8]
            return 0

        lax.fori_loop(0, rows // 8, step, 0, unroll=True)
        narrow[:, parts[h]] = wide[:, parts[h]].astype(BF16)

    def rms_of(values):
        return lax.rsqrt(jnp.mean(values * values, axis=-1, keepdims=True) + EPS)

    def gates_of(m):
        weights = routing[pl.ds(pl.multiple_of(m * tok, 8), tok), :]
        return [weights[:, 2 + k:3 + k] for k in range(2)]

    def forward_send(m):
        @pl.when(section > 0)
        def _():
            for h in range(PARTS):
                hidden_pass(m, h).wait_recv()

        values = xin[m].astype(F32)
        normed = (values * rms_of(values) * gain[...]).astype(BF16)
        table = place[0, m] + place[1, m]
        for h in range(PARTS):
            wide[:, parts[h]] = mm(table, normed[:, parts[h]])
            ship(0, m, h)

    def forward_up(m):
        @pl.when(m == 0)
        def _():
            for copy in weight_copies:
                copy.wait()

        for h in range(PARTS):
            collect(0, m, h)

            def up(n, _):
                at = pl.ds(pl.multiple_of(n * 256, 256), 256)
                pre_gate = mm(narrow[:, parts[h]], wg[parts[h], at])
                pre_up = mm(narrow[:, parts[h]], wu[parts[h], at])
                if h > 0:
                    pre_gate = kept_gate[m, :, at] + pre_gate
                    pre_up = kept_up[m, :, at] + pre_up
                kept_gate[m, :, at] = pre_gate
                kept_up[m, :, at] = pre_up
                if h == PARTS - 1:
                    inner_p[:, at] = (
                        pre_gate * jax.nn.sigmoid(pre_gate) * pre_up
                    ).astype(BF16)
                return 0

            lax.fori_loop(0, inner // 256, up, 0, unroll=True)

    def forward_down(m):
        for h in range(PARTS):
            def down(n, _):
                at = pl.ds(pl.multiple_of(h * part_width + n * 512, 512), 512)
                wide[:, at] = mm(inner_p[...], wd[:, at])
                return 0

            lax.fori_loop(0, part_width // 512, down, 0, unroll=True)
            ship(1, m, h)

    def forward_merge(m):
        gates = gates_of(m)
        for h in range(PARTS):
            collect(1, m, h)
            mixed = (
                xin[m, :, parts[h]].astype(F32)
                + gates[0] * mm(pick[0, m], narrow[:, parts[h]])
                + gates[1] * mm(pick[1, m], narrow[:, parts[h]])
            )
            hidden[m, :, parts[h]] = mixed.astype(BF16)

            @pl.when(section < sections - 1)
            def _():
                hidden_pass(m, h).start()

    def backward_send(m):
        gates = gates_of(m)
        table = jnp.concatenate(
            [place[0, m].astype(F32), place[1, m].astype(F32)], axis=1
        ).astype(BF16)
        for h in range(PARTS):
            @pl.when(section < sections - 1)
            def _():
                grads_pass(m, h).wait_recv()

            grad_out = dyin[m, :, parts[h]].astype(F32)
            scaled = jnp.concatenate(
                [(gates[k] * grad_out).astype(BF16) for k in range(2)], axis=0
            )
            wide[:, parts[h]] = mm(table, scaled)
            ship(2, m, h)

    def backward_expert(m):
        for h in range(PARTS):
            collect(2, m, h)

            def down(n, _):
                at = pl.ds(pl.multiple_of(n * 256, 256), 256)
                d_hidden = mm_last(narrow[:, parts[h]], wd[at, parts[h]])
                if h > 0:
                    d_hidden = d_inner[:, at] + d_hidden
                if h < PARTS - 1:
                    d_inner[:, at] = d_hidden
                else:
                    pre_gate = kept_gate[m, :, at]
                    pre_up = kept_up[m, :, at]
                    sigma = jax.nn.sigmoid(pre_gate)
                    inner_a[:, at] = (
                        d_hidden * pre_up * sigma * (1.0 + pre_gate * (1.0 - sigma))
                    ).astype(BF16)
                    inner_b[:, at] = (d_hidden * pre_gate * sigma).astype(BF16)
                return 0

            lax.fori_loop(0, inner // 256, down, 0, unroll=True)

        for h in range(PARTS):
            def up(n, _):
                at = pl.ds(pl.multiple_of(h * part_width + n * 512, 512), 512)
                wide[:, at] = mm_last(inner_a[...], wg[at, :]) + mm_last(inner_b[...], wu[at, :])
                return 0

            lax.fori_loop(0, part_width // 512, up, 0, unroll=True)
            ship(3, m, h)

    def backward_merge(m):
        values = xin[m].astype(F32)
        scale = rms_of(values)
        table = pick[0, m] + pick[1, m]
        weighted = []
        for h in range(PARTS):
            collect(3, m, h)
            weighted.append(mm(table, narrow[:, parts[h]]) * gain[:, parts[h]])
        total = sum(
            jnp.sum(values[:, parts[h]] * weighted[h], axis=-1, keepdims=True)
            for h in range(PARTS)
        )
        factor = scale * scale * scale * (total * (1.0 / width))
        for h in range(PARTS):
            result = (
                dyin[m, :, parts[h]].astype(F32)
                + scale * weighted[h]
                - values[:, parts[h]] * factor
            )
            grads[m, :, parts[h]] = result.astype(BF16)

            @pl.when(section > 0)
            def _():
                grads_pass(m, h).start()

    @pl.when(last)
    def _():
        def early(m, _):
            backward_send(m)
            return 0

        lax.fori_loop(0, micro, early, 0)

    def tick(t, _):
        ahead = t - section
        back = t - (2 * sections - 2 - section)
        go_ahead = (ahead >= 0) & (ahead < micro)
        go_back = (back >= 0) & (back < micro)
        others = section < sections - 1

        def guarded(condition, stage, m):
            @pl.when(condition)
            def _():
                stage(m)

        guarded(go_ahead, forward_send, ahead)
        guarded(go_ahead, forward_up, ahead)
        guarded(go_ahead & others, forward_down, ahead)
        guarded(go_back & others, backward_send, back)
        guarded(go_ahead & others, forward_merge, ahead)
        guarded(go_back, backward_expert, back)
        guarded(go_ahead & last, forward_down, ahead)
        guarded(go_back, backward_merge, back)
        guarded(go_ahead & last, forward_merge, ahead)
        return 0

    lax.fori_loop(0, 2 * sections + micro - 2, tick, 0)

    def drain(m, _):
        for h in range(PARTS):
            for kind in range(4):
                for d in range(1, experts):
                    exchange(kind, m, h, lax.rem(me + d, experts)).wait_send()

            @pl.when(section < sections - 1)
            def _():
                hidden_pass(m, h).wait_send()

            @pl.when(section > 0)
            def _():
                grads_pass(m, h).wait_send()

        return 0

    lax.fori_loop(0, micro, drain, 0)


def local(inputs, cotangent, gain, route, gate, w_gate, w_up, w_down):
    micro, tok, width = inputs.shape
    top = route.shape[-1]
    experts = lax.axis_size("expert")
    sections = lax.axis_size("section")
    capacity = tok * top * 7 // (6 * experts)
    rows = experts * capacity
    inner = w_gate.shape[-1]
    vmem = pl.BlockSpec(memory_space=pltpu.VMEM)
    hbm = pl.BlockSpec(memory_space=pl.ANY)
    shape = jax.ShapeDtypeStruct((micro, tok, width), BF16)
    routing = jnp.concatenate([route[0].astype(F32), gate[0]], axis=-1).reshape(micro * tok, 2 * top)
    hidden, grads = pl.pallas_call(
        functools.partial(kernel, experts, sections, capacity),
        out_shape=(shape, shape),
        in_specs=[vmem] * 4 + [hbm] * 3,
        out_specs=(vmem, vmem),
        scratch_shapes=[
            pltpu.VMEM((width, inner), BF16),
            pltpu.VMEM((width, inner), BF16),
            pltpu.VMEM((inner, width), BF16),
            pltpu.VMEM((micro, tok, width), BF16),
            pltpu.VMEM((micro, tok, width), BF16),
            pltpu.VMEM((4, micro, PARTS, rows * FOLD, width // PARTS // FOLD), BF16),
            pltpu.VMEM((4, micro, PARTS, rows * FOLD, width // PARTS // FOLD), BF16),
            pltpu.VMEM((micro, rows, inner), F32),
            pltpu.VMEM((micro, rows, inner), F32),
            pltpu.VMEM((rows, inner), F32),
            pltpu.VMEM((rows, width), F32),
            pltpu.VMEM((rows, width), BF16),
            pltpu.VMEM((rows, inner), BF16),
            pltpu.VMEM((rows, inner), BF16),
            pltpu.VMEM((rows, inner), BF16),
            pltpu.VMEM((2, micro, tok, rows), BF16),
            pltpu.VMEM((2, micro, rows, tok), BF16),
            pltpu.SemaphoreType.DMA((3,)),
            pltpu.SemaphoreType.DMA((4, micro, PARTS, experts)),
            pltpu.SemaphoreType.DMA((4, micro, PARTS, experts)),
            pltpu.SemaphoreType.DMA((2, micro, PARTS)),
            pltpu.SemaphoreType.DMA((2, micro, PARTS)),
        ],
        compiler_params=pltpu.CompilerParams(
            collective_id=0, has_side_effects=True, vmem_limit_bytes=60 * 2**20
        ),
    )(
        inputs, cotangent, gain, routing,
        w_gate[0, 0], w_up[0, 0], w_down[0, 0],
    )
    return (hidden[None], grads[None])


def solution(mesh):
    placed = (
        P(None, "expert", None),
        P(None, "expert", None),
        P("section", None),
        P("section", None, "expert", None),
        P("section", None, "expert", None),
        P("section", "expert", None, None),
        P("section", "expert", None, None),
        P("section", "expert", None, None),
    )
    return jax.shard_map(
        local,
        mesh=mesh,
        in_specs=placed,
        out_specs=(P("section", None, "expert", None), P("section", None, "expert", None)),
        check_vma=False,
    )
```

```python
import functools

import jax
import jax.numpy as jnp
from jax import lax
from jax.experimental import pallas as pl
from jax.experimental.pallas import tpu as pltpu
from jax.sharding import PartitionSpec as P

EPS = 1e-06
MESH = pl.DeviceIdType.MESH
FOLD = 16
PARTS = 2
F32 = jnp.float32
BF16 = jnp.bfloat16


def mm(left, right):
    return jnp.dot(left, right, preferred_element_type=F32)


def mm_last(left, right):
    return lax.dot_general(left, right, (((1,), (1,)), ((), ())), preferred_element_type=F32)


def onehot(condition):
    return jnp.where(condition, 1.0, 0.0).astype(F32)


def kernel(
    experts, sections, capacity,
    inputs, cotangent, gain, routing, w_gate, w_up, w_down,
    hidden, grads,
    wg, wu, wd, xin, dyin, sent, got, kept_gate, kept_up, d_inner, wide, narrow,
    inner_p, inner_a, inner_b, pick, place,
    weight_sem, send_sem, recv_sem, pass_send, pass_recv,
):
    micro, tok, width = inputs.shape
    inner = wg.shape[1]
    rows = experts * capacity
    block = capacity * FOLD
    part_width = width // PARTS
    piece = part_width // FOLD
    section = lax.axis_index("section")
    me = lax.axis_index("expert")
    last = section == sections - 1
    parts = [slice(h * part_width, (h + 1) * part_width) for h in range(PARTS)]

    weight_copies = [
        pltpu.make_async_copy(source, target, weight_sem.at[i])
        for i, (source, target) in enumerate(((w_gate, wg), (w_up, wu), (w_down, wd)))
    ]
    for copy in weight_copies:
        copy.start()

    barrier = pltpu.get_barrier_semaphore()
    for d in range(1, experts):
        pl.semaphore_signal(
            barrier, inc=1, device_id={"expert": lax.rem(me + d, experts)}, device_id_type=MESH
        )
    for d in (1, sections - 1):
        pl.semaphore_signal(
            barrier, inc=1, device_id={"section": lax.rem(section + d, sections)},
            device_id_type=MESH,
        )

    @pl.when(section == 0)
    def _():
        xin[...] = inputs[...]

    @pl.when(last)
    def _():
        dyin[...] = cotangent[...]

    every = micro * tok
    expert_i = lax.broadcasted_iota(jnp.int32, (every, experts), 1).astype(F32)
    ohs = [onehot(routing[:, k:k + 1] == expert_i) for k in range(2)]
    row_t = lax.broadcasted_iota(jnp.int32, (every, every), 0)
    col_t = lax.broadcasted_iota(jnp.int32, (every, every), 1)
    earlier = onehot((col_t < row_t) & (col_t // tok == row_t // tok))
    before = mm(earlier.astype(BF16), (ohs[0] + ohs[1]).astype(BF16))
    slot = lax.broadcasted_iota(jnp.int32, (every, 128), 1).astype(F32)
    for k in range(2):
        at_row = routing[:, k:k + 1] * capacity + jnp.sum(
            ohs[k] * before, axis=1, keepdims=True
        )
        table = onehot(slot == at_row)
        table_t = table.T
        for m in range(micro):
            pick[k, m] = table[m * tok:(m + 1) * tok, :rows].astype(BF16)
            place[k, m] = table_t[:rows, m * tok:(m + 1) * tok].astype(BF16)

    pl.semaphore_wait(barrier, experts + 1)

    def rows_of(e):
        return pl.ds(pl.multiple_of(e * block, 16), block)

    def exchange(kind, m, h, peer):
        return pltpu.make_async_remote_copy(
            src_ref=sent.at[kind, m, h, rows_of(peer)],
            dst_ref=got.at[kind, m, h, rows_of(me)],
            send_sem=send_sem.at[kind, m, h, peer],
            recv_sem=recv_sem.at[kind, m, h, me],
            device_id={"expert": peer},
            device_id_type=MESH,
        )

    def arrival(kind, m, h, peer):
        return pltpu.make_async_remote_copy(
            src_ref=sent.at[kind, m, h, rows_of(me)],
            dst_ref=got.at[kind, m, h, rows_of(peer)],
            send_sem=send_sem.at[kind, m, h, me],
            recv_sem=recv_sem.at[kind, m, h, peer],
            device_id={"expert": peer},
            device_id_type=MESH,
        )

    def hidden_pass(m, h):
        return pltpu.make_async_remote_copy(
            src_ref=hidden.at[m, :, parts[h]], dst_ref=xin.at[m, :, parts[h]],
            send_sem=pass_send.at[0, m, h], recv_sem=pass_recv.at[0, m, h],
            device_id={"section": lax.rem(section + 1, sections)}, device_id_type=MESH,
        )

    def grads_pass(m, h):
        return pltpu.make_async_remote_copy(
            src_ref=grads.at[m, :, parts[h]], dst_ref=dyin.at[m, :, parts[h]],
            send_sem=pass_send.at[1, m, h], recv_sem=pass_recv.at[1, m, h],
            device_id={"section": lax.rem(section + sections - 1, sections)},
            device_id_type=MESH,
        )

    span = 8 * FOLD
    row_i = lax.broadcasted_iota(jnp.int32, (span, span), 0)
    col_i = lax.broadcasted_iota(jnp.int32, (span, span), 1)

    def ship(kind, m, h):
        order = onehot(col_i == (row_i % FOLD) * 8 + row_i // FOLD).astype(BF16)

        def step(g, _):
            at = pl.ds(pl.multiple_of(g * 8, 8), 8)
            base = h * part_width
            stack = jnp.concatenate(
                [wide[at, base + p * piece:base + (p + 1) * piece] for p in range(FOLD)], axis=0
            ).astype(BF16)
            sent[kind, m, h, pl.ds(pl.multiple_of(g * span, span), span), :] = mm(
                order, stack
            ).astype(BF16)
            return 0

        lax.fori_loop(0, rows // 8, step, 0, unroll=True)
        for d in range(1, experts):
            exchange(kind, m, h, lax.rem(me + d, experts)).start()
        got[kind, m, h, rows_of(me), :] = sent[kind, m, h, rows_of(me), :]

    def collect(kind, m, h):
        for d in range(1, experts):
            arrival(kind, m, h, lax.rem(me + d, experts)).wait_recv()
        order = onehot(col_i == (row_i % 8) * FOLD + row_i // 8).astype(BF16)

        def step(g, _):
            at = pl.ds(pl.multiple_of(g * 8, 8), 8)
            base = h * part_width
            flat = mm(order, got[kind, m, h, pl.ds(pl.multiple_of(g * span, span), span), :])
            for p in range(FOLD):
                wide[at, base + p * piece:base + (p + 1) * piece] = flat[p * 8:(p + 1) * 8]
            return 0

        lax.fori_loop(0, rows // 8, step, 0, unroll=True)
        narrow[:, parts[h]] = wide[:, parts[h]].astype(BF16)

    def rms_of(values):
        return lax.rsqrt(jnp.mean(values * values, axis=-1, keepdims=True) + EPS)

    def gates_of(m):
        weights = routing[pl.ds(pl.multiple_of(m * tok, 8), tok), :]
        return [weights[:, 2 + k:3 + k] for k in range(2)]

    def forward_send(m):
        @pl.when(section > 0)
        def _():
            for h in range(PARTS):
                hidden_pass(m, h).wait_recv()

        values = xin[m].astype(F32)
        normed = (values * rms_of(values) * gain[...]).astype(BF16)
        table = place[0, m] + place[1, m]
        for h in range(PARTS):
            wide[:, parts[h]] = mm(table, normed[:, parts[h]])
            ship(0, m, h)

    def forward_up(m):
        @pl.when(m == 0)
        def _():
            for copy in weight_copies:
                copy.wait()

        for h in range(PARTS):
            collect(0, m, h)

            def up(n, _):
                at = pl.ds(pl.multiple_of(n * 256, 256), 256)
                pre_gate = mm(narrow[:, parts[h]], wg[parts[h], at])
                pre_up = mm(narrow[:, parts[h]], wu[parts[h], at])
                if h > 0:
                    pre_gate = kept_gate[m, :, at] + pre_gate
                    pre_up = kept_up[m, :, at] + pre_up
                kept_gate[m, :, at] = pre_gate
                kept_up[m, :, at] = pre_up
                if h == PARTS - 1:
                    inner_p[:, at] = (
                        pre_gate * jax.nn.sigmoid(pre_gate) * pre_up
                    ).astype(BF16)
                return 0

            lax.fori_loop(0, inner // 256, up, 0, unroll=True)

    def forward_down(m):
        for h in range(PARTS):
            def down(n, _):
                at = pl.ds(pl.multiple_of(h * part_width + n * 512, 512), 512)
                wide[:, at] = mm(inner_p[...], wd[:, at])
                return 0

            lax.fori_loop(0, part_width // 512, down, 0, unroll=True)
            ship(1, m, h)

    def forward_merge(m):
        gates = gates_of(m)
        for h in range(PARTS):
            collect(1, m, h)
            mixed = (
                xin[m, :, parts[h]].astype(F32)
                + gates[0] * mm(pick[0, m], narrow[:, parts[h]])
                + gates[1] * mm(pick[1, m], narrow[:, parts[h]])
            )
            hidden[m, :, parts[h]] = mixed.astype(BF16)

            @pl.when(section < sections - 1)
            def _():
                hidden_pass(m, h).start()

    def backward_send(m):
        gates = gates_of(m)
        table = jnp.concatenate(
            [place[0, m].astype(F32), place[1, m].astype(F32)], axis=1
        ).astype(BF16)
        for h in range(PARTS):
            @pl.when(section < sections - 1)
            def _():
                grads_pass(m, h).wait_recv()

            grad_out = dyin[m, :, parts[h]].astype(F32)
            scaled = jnp.concatenate(
                [(gates[k] * grad_out).astype(BF16) for k in range(2)], axis=0
            )
            wide[:, parts[h]] = mm(table, scaled)
            ship(2, m, h)

    def backward_expert(m):
        for h in range(PARTS):
            collect(2, m, h)

            def down(n, _):
                at = pl.ds(pl.multiple_of(n * 256, 256), 256)
                d_hidden = mm_last(narrow[:, parts[h]], wd[at, parts[h]])
                if h > 0:
                    d_hidden = d_inner[:, at] + d_hidden
                if h < PARTS - 1:
                    d_inner[:, at] = d_hidden
                else:
                    pre_gate = kept_gate[m, :, at]
                    pre_up = kept_up[m, :, at]
                    sigma = jax.nn.sigmoid(pre_gate)
                    inner_a[:, at] = (
                        d_hidden * pre_up * sigma * (1.0 + pre_gate * (1.0 - sigma))
                    ).astype(BF16)
                    inner_b[:, at] = (d_hidden * pre_gate * sigma).astype(BF16)
                return 0

            lax.fori_loop(0, inner // 256, down, 0, unroll=True)

        for h in range(PARTS):
            def up(n, _):
                at = pl.ds(pl.multiple_of(h * part_width + n * 512, 512), 512)
                wide[:, at] = mm_last(inner_a[...], wg[at, :]) + mm_last(inner_b[...], wu[at, :])
                return 0

            lax.fori_loop(0, part_width // 512, up, 0, unroll=True)
            ship(3, m, h)

    def backward_merge(m):
        values = xin[m].astype(F32)
        scale = rms_of(values)
        table = pick[0, m] + pick[1, m]
        weighted = []
        for h in range(PARTS):
            collect(3, m, h)
            weighted.append(mm(table, narrow[:, parts[h]]) * gain[:, parts[h]])
        total = sum(
            jnp.sum(values[:, parts[h]] * weighted[h], axis=-1, keepdims=True)
            for h in range(PARTS)
        )
        factor = scale * scale * scale * (total * (1.0 / width))
        for h in range(PARTS):
            result = (
                dyin[m, :, parts[h]].astype(F32)
                + scale * weighted[h]
                - values[:, parts[h]] * factor
            )
            grads[m, :, parts[h]] = result.astype(BF16)

            @pl.when(section > 0)
            def _():
                grads_pass(m, h).start()

    @pl.when(last)
    def _():
        def early(m, _):
            backward_send(m)
            return 0

        lax.fori_loop(0, micro, early, 0)

    def tick(t, _):
        ahead = t - 1
        back = jnp.where(last, ahead, ahead - micro)
        go_ahead = (ahead >= 0) & (ahead < micro)
        go_back = (back >= 0) & (back < micro)
        others = section < sections - 1

        def guarded(condition, stage, m):
            @pl.when(condition)
            def _():
                stage(m)

        guarded(go_ahead, forward_up, ahead)
        guarded(go_ahead & others, forward_down, ahead)
        guarded(go_back & others, backward_send, back)
        guarded(go_back, backward_expert, back)
        guarded(go_ahead & last, forward_down, ahead)
        guarded(t < micro, forward_send, t)
        guarded(go_back, backward_merge, back)
        guarded(go_ahead, forward_merge, ahead)
        return 0

    lax.fori_loop(0, 2 * micro + 1, tick, 0)

    def drain(m, _):
        for h in range(PARTS):
            for kind in range(4):
                for d in range(1, experts):
                    exchange(kind, m, h, lax.rem(me + d, experts)).wait_send()

            @pl.when(section < sections - 1)
            def _():
                hidden_pass(m, h).wait_send()

            @pl.when(section > 0)
            def _():
                grads_pass(m, h).wait_send()

        return 0

    lax.fori_loop(0, micro, drain, 0)


def local(inputs, cotangent, gain, route, gate, w_gate, w_up, w_down):
    micro, tok, width = inputs.shape
    top = route.shape[-1]
    experts = lax.axis_size("expert")
    sections = lax.axis_size("section")
    capacity = tok * top * 7 // (6 * experts)
    rows = experts * capacity
    inner = w_gate.shape[-1]
    vmem = pl.BlockSpec(memory_space=pltpu.VMEM)
    hbm = pl.BlockSpec(memory_space=pl.ANY)
    shape = jax.ShapeDtypeStruct((micro, tok, width), BF16)
    routing = jnp.concatenate([route[0].astype(F32), gate[0]], axis=-1).reshape(micro * tok, 2 * top)
    hidden, grads = pl.pallas_call(
        functools.partial(kernel, experts, sections, capacity),
        out_shape=(shape, shape),
        in_specs=[vmem] * 4 + [hbm] * 3,
        out_specs=(vmem, vmem),
        scratch_shapes=[
            pltpu.VMEM((width, inner), BF16),
            pltpu.VMEM((width, inner), BF16),
            pltpu.VMEM((inner, width), BF16),
            pltpu.VMEM((micro, tok, width), BF16),
            pltpu.VMEM((micro, tok, width), BF16),
            pltpu.VMEM((4, micro, PARTS, rows * FOLD, width // PARTS // FOLD), BF16),
            pltpu.VMEM((4, micro, PARTS, rows * FOLD, width // PARTS // FOLD), BF16),
            pltpu.VMEM((micro, rows, inner), F32),
            pltpu.VMEM((micro, rows, inner), F32),
            pltpu.VMEM((rows, inner), F32),
            pltpu.VMEM((rows, width), F32),
            pltpu.VMEM((rows, width), BF16),
            pltpu.VMEM((rows, inner), BF16),
            pltpu.VMEM((rows, inner), BF16),
            pltpu.VMEM((rows, inner), BF16),
            pltpu.VMEM((2, micro, tok, rows), BF16),
            pltpu.VMEM((2, micro, rows, tok), BF16),
            pltpu.SemaphoreType.DMA((3,)),
            pltpu.SemaphoreType.DMA((4, micro, PARTS, experts)),
            pltpu.SemaphoreType.DMA((4, micro, PARTS, experts)),
            pltpu.SemaphoreType.DMA((2, micro, PARTS)),
            pltpu.SemaphoreType.DMA((2, micro, PARTS)),
        ],
        compiler_params=pltpu.CompilerParams(
            collective_id=0, has_side_effects=True, vmem_limit_bytes=60 * 2**20
        ),
    )(
        inputs, cotangent, gain, routing,
        w_gate[0, 0], w_up[0, 0], w_down[0, 0],
    )
    return (hidden[None], grads[None])


def solution(mesh):
    placed = (
        P(None, "expert", None),
        P(None, "expert", None),
        P("section", None),
        P("section", None, "expert", None),
        P("section", None, "expert", None),
        P("section", "expert", None, None),
        P("section", "expert", None, None),
        P("section", "expert", None, None),
    )
    return jax.shard_map(
        local,
        mesh=mesh,
        in_specs=placed,
        out_specs=(P("section", None, "expert", None), P("section", None, "expert", None)),
        check_vma=False,
    )
```

```python
import functools

import jax
import jax.numpy as jnp
from jax import lax
from jax.experimental import pallas as pl
from jax.experimental.pallas import tpu as pltpu
from jax.sharding import PartitionSpec as P

EPS = 1e-06
MESH = pl.DeviceIdType.MESH
FOLD = 16
PARTS = 2
F32 = jnp.float32
BF16 = jnp.bfloat16


def mm(left, right):
    return jnp.dot(left, right, preferred_element_type=F32)


def mm_last(left, right):
    return lax.dot_general(left, right, (((1,), (1,)), ((), ())), preferred_element_type=F32)


def onehot(condition):
    return jnp.where(condition, 1.0, 0.0).astype(F32)


def kernel(
    experts, sections, capacity,
    inputs, cotangent, gain, routing, w_gate, w_up, w_down,
    hidden, grads,
    wg, wu, wd, xin, dyin, sent, got, kept_gate, kept_up, d_inner, wide, narrow,
    inner_p, inner_a, inner_b, pick, place,
    weight_sem, send_sem, recv_sem, pass_send, pass_recv,
):
    micro, tok, width = inputs.shape
    inner = wg.shape[1]
    rows = experts * capacity
    block = capacity * FOLD
    part_width = width // PARTS
    piece = part_width // FOLD
    section = lax.axis_index("section")
    me = lax.axis_index("expert")
    last = section == sections - 1
    parts = [slice(h * part_width, (h + 1) * part_width) for h in range(PARTS)]

    weight_copies = [
        pltpu.make_async_copy(source, target, weight_sem.at[i])
        for i, (source, target) in enumerate(((w_gate, wg), (w_up, wu), (w_down, wd)))
    ]
    for copy in weight_copies:
        copy.start()

    barrier = pltpu.get_barrier_semaphore()
    for d in range(1, experts):
        pl.semaphore_signal(
            barrier, inc=1, device_id={"expert": lax.rem(me + d, experts)}, device_id_type=MESH
        )
    for d in (1, sections - 1):
        pl.semaphore_signal(
            barrier, inc=1, device_id={"section": lax.rem(section + d, sections)},
            device_id_type=MESH,
        )

    @pl.when(section == 0)
    def _():
        xin[...] = inputs[...]

    @pl.when(last)
    def _():
        dyin[...] = cotangent[...]

    every = micro * tok
    expert_i = lax.broadcasted_iota(jnp.int32, (every, experts), 1).astype(F32)
    ohs = [onehot(routing[:, k:k + 1] == expert_i) for k in range(2)]
    row_t = lax.broadcasted_iota(jnp.int32, (every, every), 0)
    col_t = lax.broadcasted_iota(jnp.int32, (every, every), 1)
    earlier = onehot((col_t < row_t) & (col_t // tok == row_t // tok))
    before = mm(earlier.astype(BF16), (ohs[0] + ohs[1]).astype(BF16))
    slot = lax.broadcasted_iota(jnp.int32, (every, 128), 1).astype(F32)
    for k in range(2):
        at_row = routing[:, k:k + 1] * capacity + jnp.sum(
            ohs[k] * before, axis=1, keepdims=True
        )
        table = onehot(slot == at_row)
        table_t = table.T
        for m in range(micro):
            pick[k, m] = table[m * tok:(m + 1) * tok, :rows].astype(BF16)
            place[k, m] = table_t[:rows, m * tok:(m + 1) * tok].astype(BF16)

    pl.semaphore_wait(barrier, experts + 1)

    def rows_of(e):
        return pl.ds(pl.multiple_of(e * block, 16), block)

    def exchange(kind, m, h, peer):
        return pltpu.make_async_remote_copy(
            src_ref=sent.at[kind, m, h, rows_of(peer)],
            dst_ref=got.at[kind, m, h, rows_of(me)],
            send_sem=send_sem.at[kind, m, h, peer],
            recv_sem=recv_sem.at[kind, m, h, me],
            device_id={"expert": peer},
            device_id_type=MESH,
        )

    def arrival(kind, m, h, peer):
        return pltpu.make_async_remote_copy(
            src_ref=sent.at[kind, m, h, rows_of(me)],
            dst_ref=got.at[kind, m, h, rows_of(peer)],
            send_sem=send_sem.at[kind, m, h, me],
            recv_sem=recv_sem.at[kind, m, h, peer],
            device_id={"expert": peer},
            device_id_type=MESH,
        )

    def hidden_pass(m, h):
        return pltpu.make_async_remote_copy(
            src_ref=hidden.at[m, :, parts[h]], dst_ref=xin.at[m, :, parts[h]],
            send_sem=pass_send.at[0, m, h], recv_sem=pass_recv.at[0, m, h],
            device_id={"section": lax.rem(section + 1, sections)}, device_id_type=MESH,
        )

    def grads_pass(m, h):
        return pltpu.make_async_remote_copy(
            src_ref=grads.at[m, :, parts[h]], dst_ref=dyin.at[m, :, parts[h]],
            send_sem=pass_send.at[1, m, h], recv_sem=pass_recv.at[1, m, h],
            device_id={"section": lax.rem(section + sections - 1, sections)},
            device_id_type=MESH,
        )

    span = 8 * FOLD
    row_i = lax.broadcasted_iota(jnp.int32, (span, span), 0)
    col_i = lax.broadcasted_iota(jnp.int32, (span, span), 1)

    def ship(kind, m, h):
        order = onehot(col_i == (row_i % FOLD) * 8 + row_i // FOLD).astype(BF16)

        def step(g, _):
            at = pl.ds(pl.multiple_of(g * 8, 8), 8)
            base = h * part_width
            stack = jnp.concatenate(
                [wide[at, base + p * piece:base + (p + 1) * piece] for p in range(FOLD)], axis=0
            ).astype(BF16)
            sent[kind, m, h, pl.ds(pl.multiple_of(g * span, span), span), :] = mm(
                order, stack
            ).astype(BF16)
            return 0

        lax.fori_loop(0, rows // 8, step, 0, unroll=True)
        for d in range(1, experts):
            exchange(kind, m, h, lax.rem(me + d, experts)).start()
        got[kind, m, h, rows_of(me), :] = sent[kind, m, h, rows_of(me), :]

    def collect(kind, m, h):
        for d in range(1, experts):
            arrival(kind, m, h, lax.rem(me + d, experts)).wait_recv()
        order = onehot(col_i == (row_i % 8) * FOLD + row_i // 8).astype(BF16)

        def step(g, _):
            at = pl.ds(pl.multiple_of(g * 8, 8), 8)
            base = h * part_width
            flat = mm(order, got[kind, m, h, pl.ds(pl.multiple_of(g * span, span), span), :])
            for p in range(FOLD):
                wide[at, base + p * piece:base + (p + 1) * piece] = flat[p * 8:(p + 1) * 8]
            return 0

        lax.fori_loop(0, rows // 8, step, 0, unroll=True)
        narrow[:, parts[h]] = wide[:, parts[h]].astype(BF16)

    def rms_of(values):
        return lax.rsqrt(jnp.mean(values * values, axis=-1, keepdims=True) + EPS)

    def gates_of(m):
        weights = routing[pl.ds(pl.multiple_of(m * tok, 8), tok), :]
        return [weights[:, 2 + k:3 + k] for k in range(2)]

    def forward_send(m):
        @pl.when(section > 0)
        def _():
            for h in range(PARTS):
                hidden_pass(m, h).wait_recv()

        values = xin[m].astype(F32)
        normed = (values * rms_of(values) * gain[...]).astype(BF16)
        table = place[0, m] + place[1, m]
        for h in range(PARTS):
            wide[:, parts[h]] = mm(table, normed[:, parts[h]])
            ship(0, m, h)

    def forward_up(m):
        @pl.when(m == 0)
        def _():
            for copy in weight_copies:
                copy.wait()

        for h in range(PARTS):
            collect(0, m, h)

            def up(n, _):
                at = pl.ds(pl.multiple_of(n * 256, 256), 256)
                pre_gate = mm(narrow[:, parts[h]], wg[parts[h], at])
                pre_up = mm(narrow[:, parts[h]], wu[parts[h], at])
                if h > 0:
                    pre_gate = kept_gate[m, :, at] + pre_gate
                    pre_up = kept_up[m, :, at] + pre_up
                kept_gate[m, :, at] = pre_gate
                kept_up[m, :, at] = pre_up
                if h == PARTS - 1:
                    inner_p[:, at] = (
                        pre_gate * jax.nn.sigmoid(pre_gate) * pre_up
                    ).astype(BF16)
                return 0

            lax.fori_loop(0, inner // 256, up, 0, unroll=True)

    def forward_down(m):
        for h in range(PARTS):
            def down(n, _):
                at = pl.ds(pl.multiple_of(h * part_width + n * 512, 512), 512)
                wide[:, at] = mm(inner_p[...], wd[:, at])
                return 0

            lax.fori_loop(0, part_width // 512, down, 0, unroll=True)
            ship(1, m, h)

    def forward_merge(m):
        gates = gates_of(m)
        for h in range(PARTS):
            collect(1, m, h)
            mixed = (
                xin[m, :, parts[h]].astype(F32)
                + gates[0] * mm(pick[0, m], narrow[:, parts[h]])
                + gates[1] * mm(pick[1, m], narrow[:, parts[h]])
            )
            hidden[m, :, parts[h]] = mixed.astype(BF16)

            @pl.when(section < sections - 1)
            def _():
                hidden_pass(m, h).start()

    def backward_send(m):
        gates = gates_of(m)
        table = jnp.concatenate(
            [place[0, m].astype(F32), place[1, m].astype(F32)], axis=1
        ).astype(BF16)
        for h in range(PARTS):
            @pl.when(section < sections - 1)
            def _():
                grads_pass(m, h).wait_recv()

            grad_out = dyin[m, :, parts[h]].astype(F32)
            scaled = jnp.concatenate(
                [(gates[k] * grad_out).astype(BF16) for k in range(2)], axis=0
            )
            wide[:, parts[h]] = mm(table, scaled)
            ship(2, m, h)

    def backward_expert(m):
        for h in range(PARTS):
            collect(2, m, h)

            def down(n, _):
                at = pl.ds(pl.multiple_of(n * 256, 256), 256)
                d_hidden = mm_last(narrow[:, parts[h]], wd[at, parts[h]])
                if h > 0:
                    d_hidden = d_inner[:, at] + d_hidden
                if h < PARTS - 1:
                    d_inner[:, at] = d_hidden
                else:
                    pre_gate = kept_gate[m, :, at]
                    pre_up = kept_up[m, :, at]
                    sigma = jax.nn.sigmoid(pre_gate)
                    inner_a[:, at] = (
                        d_hidden * pre_up * sigma * (1.0 + pre_gate * (1.0 - sigma))
                    ).astype(BF16)
                    inner_b[:, at] = (d_hidden * pre_gate * sigma).astype(BF16)
                return 0

            lax.fori_loop(0, inner // 256, down, 0, unroll=True)

        for h in range(PARTS):
            def up(n, _):
                at = pl.ds(pl.multiple_of(h * part_width + n * 512, 512), 512)
                wide[:, at] = mm_last(inner_a[...], wg[at, :]) + mm_last(inner_b[...], wu[at, :])
                return 0

            lax.fori_loop(0, part_width // 512, up, 0, unroll=True)
            ship(3, m, h)

    def backward_merge(m):
        values = xin[m].astype(F32)
        scale = rms_of(values)
        table = pick[0, m] + pick[1, m]
        weighted = []
        for h in range(PARTS):
            collect(3, m, h)
            weighted.append(mm(table, narrow[:, parts[h]]) * gain[:, parts[h]])
        total = sum(
            jnp.sum(values[:, parts[h]] * weighted[h], axis=-1, keepdims=True)
            for h in range(PARTS)
        )
        factor = scale * scale * scale * (total * (1.0 / width))
        for h in range(PARTS):
            result = (
                dyin[m, :, parts[h]].astype(F32)
                + scale * weighted[h]
                - values[:, parts[h]] * factor
            )
            grads[m, :, parts[h]] = result.astype(BF16)

            @pl.when(section > 0)
            def _():
                grads_pass(m, h).start()

    @pl.when(last)
    def _():
        def early(m, _):
            backward_send(m)
            return 0

        lax.fori_loop(0, micro, early, 0)

    def tick(t, _):
        ahead = t - section
        back = t - (2 * sections - 2 - section)
        go_ahead = (ahead >= 0) & (ahead < micro)
        go_back = (back >= 0) & (back < micro)
        others = section < sections - 1

        def guarded(condition, stage, m):
            @pl.when(condition)
            def _():
                stage(m)

        guarded(go_ahead & others, forward_send, ahead)
        guarded(go_ahead, forward_up, ahead)
        guarded(go_ahead & others, forward_down, ahead)
        guarded(go_back & others, backward_send, back)
        guarded(go_ahead & others, forward_merge, ahead)
        guarded(go_back, backward_expert, back)
        guarded(go_ahead & last, forward_down, ahead)
        guarded((ahead >= -1) & (ahead < micro - 1) & last, forward_send, ahead + 1)
        guarded(go_back, backward_merge, back)
        guarded(go_ahead & last, forward_merge, ahead)
        return 0

    lax.fori_loop(0, 2 * sections + micro - 2, tick, 0)

    def drain(m, _):
        for h in range(PARTS):
            for kind in range(4):
                for d in range(1, experts):
                    exchange(kind, m, h, lax.rem(me + d, experts)).wait_send()

            @pl.when(section < sections - 1)
            def _():
                hidden_pass(m, h).wait_send()

            @pl.when(section > 0)
            def _():
                grads_pass(m, h).wait_send()

        return 0

    lax.fori_loop(0, micro, drain, 0)


def local(inputs, cotangent, gain, route, gate, w_gate, w_up, w_down):
    micro, tok, width = inputs.shape
    top = route.shape[-1]
    experts = lax.axis_size("expert")
    sections = lax.axis_size("section")
    capacity = tok * top * 7 // (6 * experts)
    rows = experts * capacity
    inner = w_gate.shape[-1]
    vmem = pl.BlockSpec(memory_space=pltpu.VMEM)
    hbm = pl.BlockSpec(memory_space=pl.ANY)
    shape = jax.ShapeDtypeStruct((micro, tok, width), BF16)
    routing = jnp.concatenate([route[0].astype(F32), gate[0]], axis=-1).reshape(micro * tok, 2 * top)
    hidden, grads = pl.pallas_call(
        functools.partial(kernel, experts, sections, capacity),
        out_shape=(shape, shape),
        in_specs=[vmem] * 4 + [hbm] * 3,
        out_specs=(vmem, vmem),
        scratch_shapes=[
            pltpu.VMEM((width, inner), BF16),
            pltpu.VMEM((width, inner), BF16),
            pltpu.VMEM((inner, width), BF16),
            pltpu.VMEM((micro, tok, width), BF16),
            pltpu.VMEM((micro, tok, width), BF16),
            pltpu.VMEM((4, micro, PARTS, rows * FOLD, width // PARTS // FOLD), BF16),
            pltpu.VMEM((4, micro, PARTS, rows * FOLD, width // PARTS // FOLD), BF16),
            pltpu.VMEM((micro, rows, inner), F32),
            pltpu.VMEM((micro, rows, inner), F32),
            pltpu.VMEM((rows, inner), F32),
            pltpu.VMEM((rows, width), F32),
            pltpu.VMEM((rows, width), BF16),
            pltpu.VMEM((rows, inner), BF16),
            pltpu.VMEM((rows, inner), BF16),
            pltpu.VMEM((rows, inner), BF16),
            pltpu.VMEM((2, micro, tok, rows), BF16),
            pltpu.VMEM((2, micro, rows, tok), BF16),
            pltpu.SemaphoreType.DMA((3,)),
            pltpu.SemaphoreType.DMA((4, micro, PARTS, experts)),
            pltpu.SemaphoreType.DMA((4, micro, PARTS, experts)),
            pltpu.SemaphoreType.DMA((2, micro, PARTS)),
            pltpu.SemaphoreType.DMA((2, micro, PARTS)),
        ],
        compiler_params=pltpu.CompilerParams(
            collective_id=0, has_side_effects=True, vmem_limit_bytes=60 * 2**20
        ),
    )(
        inputs, cotangent, gain, routing,
        w_gate[0, 0], w_up[0, 0], w_down[0, 0],
    )
    return (hidden[None], grads[None])


def solution(mesh):
    placed = (
        P(None, "expert", None),
        P(None, "expert", None),
        P("section", None),
        P("section", None, "expert", None),
        P("section", None, "expert", None),
        P("section", "expert", None, None),
        P("section", "expert", None, None),
        P("section", "expert", None, None),
    )
    return jax.shard_map(
        local,
        mesh=mesh,
        in_specs=placed,
        out_specs=(P("section", None, "expert", None), P("section", None, "expert", None)),
        check_vma=False,
    )
```

```python
import functools

import jax
import jax.numpy as jnp
from jax import lax
from jax.experimental import pallas as pl
from jax.experimental.pallas import tpu as pltpu
from jax.sharding import PartitionSpec as P

EPS = 1e-06
MESH = pl.DeviceIdType.MESH
FOLD = 16
PARTS = 2
F32 = jnp.float32
BF16 = jnp.bfloat16


def mm(left, right):
    return jnp.dot(left, right, preferred_element_type=F32)


def mm_last(left, right):
    return lax.dot_general(left, right, (((1,), (1,)), ((), ())), preferred_element_type=F32)


def onehot(condition):
    return jnp.where(condition, 1.0, 0.0).astype(F32)


def kernel(
    experts, sections, capacity,
    inputs, cotangent, gain, routing, w_gate, w_up, w_down,
    hidden, grads,
    wg, wu, wd, xin, dyin, sent, got, kept_gate, kept_up, d_inner, wide, narrow,
    inner_p, inner_a, inner_b, pick, place,
    weight_sem, send_sem, recv_sem, pass_send, pass_recv,
):
    micro, tok, width = inputs.shape
    inner = wg.shape[1]
    rows = experts * capacity
    block = capacity * FOLD
    part_width = width // PARTS
    piece = part_width // FOLD
    section = lax.axis_index("section")
    me = lax.axis_index("expert")
    last = section == sections - 1
    parts = [slice(h * part_width, (h + 1) * part_width) for h in range(PARTS)]

    weight_copies = [
        pltpu.make_async_copy(source, target, weight_sem.at[i])
        for i, (source, target) in enumerate(((w_gate, wg), (w_up, wu), (w_down, wd)))
    ]
    for copy in weight_copies:
        copy.start()

    barrier = pltpu.get_barrier_semaphore()
    for d in range(1, experts):
        pl.semaphore_signal(
            barrier, inc=1, device_id={"expert": lax.rem(me + d, experts)}, device_id_type=MESH
        )
    for d in (1, sections - 1):
        pl.semaphore_signal(
            barrier, inc=1, device_id={"section": lax.rem(section + d, sections)},
            device_id_type=MESH,
        )

    @pl.when(section == 0)
    def _():
        xin[...] = inputs[...]

    @pl.when(last)
    def _():
        dyin[...] = cotangent[...]

    every = micro * tok
    expert_i = lax.broadcasted_iota(jnp.int32, (every, experts), 1).astype(F32)
    ohs = [onehot(routing[:, k:k + 1] == expert_i) for k in range(2)]
    row_t = lax.broadcasted_iota(jnp.int32, (every, every), 0)
    col_t = lax.broadcasted_iota(jnp.int32, (every, every), 1)
    earlier = onehot((col_t < row_t) & (col_t // tok == row_t // tok))
    before = mm(earlier.astype(BF16), (ohs[0] + ohs[1]).astype(BF16))
    slot = lax.broadcasted_iota(jnp.int32, (every, 128), 1).astype(F32)
    for k in range(2):
        at_row = routing[:, k:k + 1] * capacity + jnp.sum(
            ohs[k] * before, axis=1, keepdims=True
        )
        table = onehot(slot == at_row)
        table_t = table.T
        for m in range(micro):
            pick[k, m] = table[m * tok:(m + 1) * tok, :rows].astype(BF16)
            place[k, m] = table_t[:rows, m * tok:(m + 1) * tok].astype(BF16)

    pl.semaphore_wait(barrier, experts + 1)

    def rows_of(e):
        return pl.ds(pl.multiple_of(e * block, 16), block)

    def exchange(kind, m, h, peer):
        return pltpu.make_async_remote_copy(
            src_ref=sent.at[kind, m, h, rows_of(peer)],
            dst_ref=got.at[kind, m, h, rows_of(me)],
            send_sem=send_sem.at[kind, m, h, peer],
            recv_sem=recv_sem.at[kind, m, h, me],
            device_id={"expert": peer},
            device_id_type=MESH,
        )

    def arrival(kind, m, h, peer):
        return pltpu.make_async_remote_copy(
            src_ref=sent.at[kind, m, h, rows_of(me)],
            dst_ref=got.at[kind, m, h, rows_of(peer)],
            send_sem=send_sem.at[kind, m, h, me],
            recv_sem=recv_sem.at[kind, m, h, peer],
            device_id={"expert": peer},
            device_id_type=MESH,
        )

    def hidden_pass(m, h):
        return pltpu.make_async_remote_copy(
            src_ref=hidden.at[m, :, parts[h]], dst_ref=xin.at[m, :, parts[h]],
            send_sem=pass_send.at[0, m, h], recv_sem=pass_recv.at[0, m, h],
            device_id={"section": lax.rem(section + 1, sections)}, device_id_type=MESH,
        )

    def grads_pass(m, h):
        return pltpu.make_async_remote_copy(
            src_ref=grads.at[m, :, parts[h]], dst_ref=dyin.at[m, :, parts[h]],
            send_sem=pass_send.at[1, m, h], recv_sem=pass_recv.at[1, m, h],
            device_id={"section": lax.rem(section + sections - 1, sections)},
            device_id_type=MESH,
        )

    span = 8 * FOLD
    row_i = lax.broadcasted_iota(jnp.int32, (span, span), 0)
    col_i = lax.broadcasted_iota(jnp.int32, (span, span), 1)

    def ship(kind, m, h):
        order = onehot(col_i == (row_i % FOLD) * 8 + row_i // FOLD).astype(BF16)

        def step(g, _):
            at = pl.ds(pl.multiple_of(g * 8, 8), 8)
            base = h * part_width
            stack = jnp.concatenate(
                [wide[at, base + p * piece:base + (p + 1) * piece] for p in range(FOLD)], axis=0
            ).astype(BF16)
            sent[kind, m, h, pl.ds(pl.multiple_of(g * span, span), span), :] = mm(
                order, stack
            ).astype(BF16)
            return 0

        lax.fori_loop(0, rows // 8, step, 0, unroll=True)
        for d in range(1, experts):
            exchange(kind, m, h, lax.rem(me + d, experts)).start()
        got[kind, m, h, rows_of(me), :] = sent[kind, m, h, rows_of(me), :]

    def collect(kind, m, h):
        for d in range(1, experts):
            arrival(kind, m, h, lax.rem(me + d, experts)).wait_recv()
        order = onehot(col_i == (row_i % 8) * FOLD + row_i // 8).astype(BF16)

        def step(g, _):
            at = pl.ds(pl.multiple_of(g * 8, 8), 8)
            base = h * part_width
            flat = mm(order, got[kind, m, h, pl.ds(pl.multiple_of(g * span, span), span), :])
            for p in range(FOLD):
                wide[at, base + p * piece:base + (p + 1) * piece] = flat[p * 8:(p + 1) * 8]
            return 0

        lax.fori_loop(0, rows // 8, step, 0, unroll=True)
        narrow[:, parts[h]] = wide[:, parts[h]].astype(BF16)

    def rms_of(values):
        return lax.rsqrt(jnp.mean(values * values, axis=-1, keepdims=True) + EPS)

    def gates_of(m):
        weights = routing[pl.ds(pl.multiple_of(m * tok, 8), tok), :]
        return [weights[:, 2 + k:3 + k] for k in range(2)]

    def forward_send(m):
        @pl.when(section > 0)
        def _():
            for h in range(PARTS):
                hidden_pass(m, h).wait_recv()

        values = xin[m].astype(F32)
        normed = (values * rms_of(values) * gain[...]).astype(BF16)
        table = place[0, m] + place[1, m]
        for h in range(PARTS):
            wide[:, parts[h]] = mm(table, normed[:, parts[h]])
            ship(0, m, h)

    def forward_up(m):
        @pl.when(m == 0)
        def _():
            for copy in weight_copies:
                copy.wait()

        for h in range(PARTS):
            collect(0, m, h)

            def up(n, _):
                at = pl.ds(pl.multiple_of(n * 256, 256), 256)
                pre_gate = mm(narrow[:, parts[h]], wg[parts[h], at])
                pre_up = mm(narrow[:, parts[h]], wu[parts[h], at])
                if h > 0:
                    pre_gate = kept_gate[m, :, at] + pre_gate
                    pre_up = kept_up[m, :, at] + pre_up
                kept_gate[m, :, at] = pre_gate
                kept_up[m, :, at] = pre_up
                if h == PARTS - 1:
                    inner_p[:, at] = (
                        pre_gate * jax.nn.sigmoid(pre_gate) * pre_up
                    ).astype(BF16)
                return 0

            lax.fori_loop(0, inner // 256, up, 0, unroll=True)

    def forward_down(m):
        for h in range(PARTS):
            def down(n, _):
                at = pl.ds(pl.multiple_of(h * part_width + n * 512, 512), 512)
                wide[:, at] = mm(inner_p[...], wd[:, at])
                return 0

            lax.fori_loop(0, part_width // 512, down, 0, unroll=True)
            ship(1, m, h)

    def forward_merge(m):
        gates = gates_of(m)
        for h in range(PARTS):
            collect(1, m, h)
            mixed = (
                xin[m, :, parts[h]].astype(F32)
                + gates[0] * mm(pick[0, m], narrow[:, parts[h]])
                + gates[1] * mm(pick[1, m], narrow[:, parts[h]])
            )
            hidden[m, :, parts[h]] = mixed.astype(BF16)

            @pl.when(section < sections - 1)
            def _():
                hidden_pass(m, h).start()

    def backward_send(m):
        gates = gates_of(m)
        table = jnp.concatenate(
            [place[0, m].astype(F32), place[1, m].astype(F32)], axis=1
        ).astype(BF16)
        for h in range(PARTS):
            @pl.when(section < sections - 1)
            def _():
                grads_pass(m, h).wait_recv()

            grad_out = dyin[m, :, parts[h]].astype(F32)
            scaled = jnp.concatenate(
                [(gates[k] * grad_out).astype(BF16) for k in range(2)], axis=0
            )
            wide[:, parts[h]] = mm(table, scaled)
            ship(2, m, h)

    def backward_expert(m):
        for h in range(PARTS):
            collect(2, m, h)

            def down(n, _):
                at = pl.ds(pl.multiple_of(n * 256, 256), 256)
                d_hidden = mm_last(narrow[:, parts[h]], wd[at, parts[h]])
                if h > 0:
                    d_hidden = d_inner[:, at] + d_hidden
                if h < PARTS - 1:
                    d_inner[:, at] = d_hidden
                else:
                    pre_gate = kept_gate[m, :, at]
                    pre_up = kept_up[m, :, at]
                    sigma = jax.nn.sigmoid(pre_gate)
                    inner_a[:, at] = (
                        d_hidden * pre_up * sigma * (1.0 + pre_gate * (1.0 - sigma))
                    ).astype(BF16)
                    inner_b[:, at] = (d_hidden * pre_gate * sigma).astype(BF16)
                return 0

            lax.fori_loop(0, inner // 256, down, 0, unroll=True)

        for h in range(PARTS):
            def up(n, _):
                at = pl.ds(pl.multiple_of(h * part_width + n * 512, 512), 512)
                wide[:, at] = mm_last(inner_a[...], wg[at, :]) + mm_last(inner_b[...], wu[at, :])
                return 0

            lax.fori_loop(0, part_width // 512, up, 0, unroll=True)
            ship(3, m, h)

    def backward_merge(m):
        values = xin[m].astype(F32)
        scale = rms_of(values)
        table = pick[0, m] + pick[1, m]
        weighted = []
        for h in range(PARTS):
            collect(3, m, h)
            weighted.append(mm(table, narrow[:, parts[h]]) * gain[:, parts[h]])
        total = sum(
            jnp.sum(values[:, parts[h]] * weighted[h], axis=-1, keepdims=True)
            for h in range(PARTS)
        )
        factor = scale * scale * scale * (total * (1.0 / width))
        for h in range(PARTS):
            result = (
                dyin[m, :, parts[h]].astype(F32)
                + scale * weighted[h]
                - values[:, parts[h]] * factor
            )
            grads[m, :, parts[h]] = result.astype(BF16)

            @pl.when(section > 0)
            def _():
                grads_pass(m, h).start()

    @pl.when(last)
    def _():
        def early(m, _):
            backward_send(m)
            return 0

        lax.fori_loop(0, micro, early, 0)

    def tick(t, _):
        ahead = t - section
        back = jnp.where(last, ahead, ahead - micro)
        go_ahead = (ahead >= 0) & (ahead < micro)
        go_back = (back >= 0) & (back < micro)
        others = section < sections - 1

        def guarded(condition, stage, m):
            @pl.when(condition)
            def _():
                stage(m)

        guarded(go_ahead & others, forward_send, ahead)
        guarded(go_ahead, forward_up, ahead)
        guarded(go_ahead & others, forward_down, ahead)
        guarded(go_back & others, backward_send, back)
        guarded(go_ahead & others, forward_merge, ahead)
        guarded(go_back, backward_expert, back)
        guarded(go_ahead & last, forward_down, ahead)
        guarded((ahead >= -1) & (ahead < micro - 1) & last, forward_send, ahead + 1)
        guarded(go_back, backward_merge, back)
        guarded(go_ahead & last, forward_merge, ahead)
        return 0

    lax.fori_loop(0, sections - 1 + 2 * micro, tick, 0)

    def drain(m, _):
        for h in range(PARTS):
            for kind in range(4):
                for d in range(1, experts):
                    exchange(kind, m, h, lax.rem(me + d, experts)).wait_send()

            @pl.when(section < sections - 1)
            def _():
                hidden_pass(m, h).wait_send()

            @pl.when(section > 0)
            def _():
                grads_pass(m, h).wait_send()

        return 0

    lax.fori_loop(0, micro, drain, 0)


def place_outputs(hidden, grads, hidden_out, grads_out, sem):
    copies = [
        pltpu.make_async_copy(hidden, hidden_out, sem.at[0]),
        pltpu.make_async_copy(grads, grads_out, sem.at[1]),
    ]
    for copy in copies:
        copy.start()
    for copy in copies:
        copy.wait()


def local(inputs, cotangent, gain, route, gate, w_gate, w_up, w_down):
    micro, tok, width = inputs.shape
    top = route.shape[-1]
    experts = lax.axis_size("expert")
    sections = lax.axis_size("section")
    capacity = tok * top * 7 // (6 * experts)
    rows = experts * capacity
    inner = w_gate.shape[-1]
    vmem = pl.BlockSpec(memory_space=pltpu.VMEM)
    hbm = pl.BlockSpec(memory_space=pl.ANY)
    shape = jax.ShapeDtypeStruct((micro, tok, width), BF16)
    routing = jnp.concatenate([route[0].astype(F32), gate[0]], axis=-1).reshape(micro * tok, 2 * top)
    hidden, grads = pl.pallas_call(
        functools.partial(kernel, experts, sections, capacity),
        out_shape=(shape, shape),
        in_specs=[vmem] * 4 + [hbm] * 3,
        out_specs=(vmem, vmem),
        scratch_shapes=[
            pltpu.VMEM((width, inner), BF16),
            pltpu.VMEM((width, inner), BF16),
            pltpu.VMEM((inner, width), BF16),
            pltpu.VMEM((micro, tok, width), BF16),
            pltpu.VMEM((micro, tok, width), BF16),
            pltpu.VMEM((4, micro, PARTS, rows * FOLD, width // PARTS // FOLD), BF16),
            pltpu.VMEM((4, micro, PARTS, rows * FOLD, width // PARTS // FOLD), BF16),
            pltpu.VMEM((micro, rows, inner), F32),
            pltpu.VMEM((micro, rows, inner), F32),
            pltpu.VMEM((rows, inner), F32),
            pltpu.VMEM((rows, width), F32),
            pltpu.VMEM((rows, width), BF16),
            pltpu.VMEM((rows, inner), BF16),
            pltpu.VMEM((rows, inner), BF16),
            pltpu.VMEM((rows, inner), BF16),
            pltpu.VMEM((2, micro, tok, rows), BF16),
            pltpu.VMEM((2, micro, rows, tok), BF16),
            pltpu.SemaphoreType.DMA((3,)),
            pltpu.SemaphoreType.DMA((4, micro, PARTS, experts)),
            pltpu.SemaphoreType.DMA((4, micro, PARTS, experts)),
            pltpu.SemaphoreType.DMA((2, micro, PARTS)),
            pltpu.SemaphoreType.DMA((2, micro, PARTS)),
        ],
        compiler_params=pltpu.CompilerParams(
            collective_id=0, has_side_effects=True, vmem_limit_bytes=60 * 2**20
        ),
    )(
        inputs, cotangent, gain, routing,
        w_gate[0, 0], w_up[0, 0], w_down[0, 0],
    )
    hidden, grads = pl.pallas_call(
        place_outputs,
        out_shape=(shape, shape),
        in_specs=[hbm] * 2,
        out_specs=(hbm, hbm),
        scratch_shapes=[pltpu.SemaphoreType.DMA((2,))],
    )(hidden, grads)
    return (hidden[None], grads[None])


def solution(mesh):
    placed = (
        P(None, "expert", None),
        P(None, "expert", None),
        P("section", None),
        P("section", None, "expert", None),
        P("section", None, "expert", None),
        P("section", "expert", None, None),
        P("section", "expert", None, None),
        P("section", "expert", None, None),
    )
    return jax.shard_map(
        local,
        mesh=mesh,
        in_specs=placed,
        out_specs=(P("section", None, "expert", None), P("section", None, "expert", None)),
        check_vma=False,
    )
```
